512 devices in a mesh: fsdp: 64 (over y, z), mat: 8 (over x, core).
Axes of the slice: x: 4, y: 4, z: 16, core: 2. Of those that a mesh axis runs over, the one named last changes fastest.
Arguments:
- momentum: bfloat16 [16384, 16384], P('fsdp', 'mat'), may hold values from -32 to 32
- gradient: bfloat16 [16384, 16384], P('fsdp', 'mat'), may hold values from -6 to 6
- right_factor: float32 [16384, 128], P(('mat', 'fsdp')), may hold values from -6 to 6
Outputs:
- new_momentum: bfloat16 [16384, 16384], P('fsdp', 'mat')
- update: bfloat16 [16384, 16384], P('fsdp', 'mat')
- new_right: float32 [16384, 128], P(('mat', 'fsdp'))
The draws below stay inside these ranges and needn't reach their ends.
All inputs are finite; a program needn't handle non-finite values.
Results may differ from the reference program's by a relative error of at most 0.012.
Values may be sent and summed in bfloat16 or wider, within the bound.
A program may use at most 64 MiB of HBM per device.

```python
import math
import jax
import jax.numpy as jnp
from jax import lax

D = 16384
RANK = 128


def draw_momentum(key, part):
    key = jax.random.fold_in(key, 11)
    keys = jax.random.split(key, 5)
    noise_part = jax.random.truncated_normal(keys[0], -4.0, 4.0, (D, D), jnp.float32)
    row_scale = jnp.exp(jax.random.uniform(keys[1], (D, 1), jnp.float32) * 0.6931)
    ramp = jnp.sqrt(1.0 + 2.0 * jnp.arange(D, dtype=jnp.float32) / D)
    col_scale = jnp.exp(jax.random.uniform(keys[2], (1, D), jnp.float32) * 0.6931) * ramp[None, :]
    left_vec = jax.random.uniform(keys[3], (D, 1), jnp.float32, -2.0, 2.0)
    right_vec = jax.random.uniform(keys[4], (1, D), jnp.float32, -2.0, 2.0)
    return (noise_part * row_scale * col_scale + left_vec * right_vec).astype(jnp.bfloat16)


def shard_levels(rng, shape, pieces, smallest, largest):
    level, own = 1.0, jax.random.fold_in(rng, 6)
    for axis_at, parts in pieces:
        steps = jnp.exp(jax.random.uniform(jax.random.fold_in(own, axis_at), (parts,), jnp.float32, smallest / len(pieces), largest / len(pieces)))
        level = level * jnp.repeat(steps, shape[axis_at] // parts).reshape([-1 if axis == axis_at else 1 for axis in range(len(shape))])
    return level


def centred(own_key, extent, scale, limit, pieces=(), held_as=jnp.bfloat16):
    array = jax.random.normal(own_key, extent, jnp.float32) * scale
    if len(pieces) > 0:
        array = shard_levels(own_key, extent, pieces, -0.22, 0.18) * array
    return jnp.clip(array, min=-limit, max=limit).astype(held_as)


def setup_inputs(seed: int = 0) -> dict:
    streams_of = jax.random.split(jax.random.key(seed), 4)
    return {
        "momentum": draw_momentum(jax.random.fold_in(streams_of[3], 71), 0),
        "gradient": centred(streams_of[1], (D, D), 1.0, 6.0, ((0, 64), (1, 8))),
        "right_factor": centred(streams_of[2], (D, RANK), 1.0, 6.0, ((0, 512),), jnp.float32),
    }


keep_factor = 0.95
norm_eps = 1e-06

def reference(momentum, gradient, right_factor):
    buffer = (momentum.astype(jnp.float32) + gradient.astype(jnp.float32)).astype(jnp.bfloat16)
    right_bf = right_factor.astype(jnp.bfloat16)
    projected = jnp.dot(buffer.astype(jnp.float32), right_bf.astype(jnp.float32), preferred_element_type=jnp.float32)
    gram = jnp.dot(projected.T, projected, precision=lax.Precision.HIGHEST)
    factor_low = jnp.linalg.cholesky(gram)
    orthonormal = lax.linalg.triangular_solve(factor_low, projected, left_side=False, lower=True, transpose_a=True)
    orth_bf = orthonormal.astype(jnp.bfloat16)
    columns = lax.dot_general(buffer.astype(jnp.float32), orth_bf.astype(jnp.float32), (((0,), (0,)), ((), ())), preferred_element_type=jnp.float32)
    sumsq = lax.optimization_barrier(jnp.sum(columns * columns, axis=0))
    new_right = math.sqrt(D) * columns * lax.rsqrt(sumsq + norm_eps)
    columns_bf = columns.astype(jnp.bfloat16)
    right_new_bf = new_right.astype(jnp.bfloat16)
    feedback = jnp.dot(orth_bf.astype(jnp.float32), columns_bf.T.astype(jnp.float32), preferred_element_type=jnp.float32)
    new_momentum = (buffer.astype(jnp.float32) - (1.0 - keep_factor) * feedback).astype(jnp.bfloat16)
    update = (math.sqrt(D / RANK) * jnp.dot(orth_bf.astype(jnp.float32), right_new_bf.T.astype(jnp.float32), preferred_element_type=jnp.float32)).astype(jnp.bfloat16)
    return (new_momentum, update, new_right)
```

```python
import functools
import math

import jax
import jax.numpy as jnp
from jax import lax
from jax.experimental import pallas as pl
from jax.experimental.pallas import tpu as pltpu
from jax.sharding import PartitionSpec as P

D = 16384
RANK = 128
Y, Z = 4, 16

keep_factor = 0.95
norm_eps = 1e-06

MESH = pl.DeviceIdType.MESH
F32, BF16 = jnp.float32, jnp.bfloat16
HIGH = lax.Precision.HIGHEST
BLOCK = 16


def distance(i):
    half = (i + 1) // 2
    odd = i % 2
    return half * odd + (Z - half) * (1 - odd)


def factor_inverse(a_ref, v_ref):
    n = a_ref.shape[0]
    rows = lax.broadcasted_iota(jnp.int32, (n, n), 0)
    lanes = lax.broadcasted_iota(jnp.int32, (n, n), 1)
    v_ref[...] = jnp.where(rows == lanes, 1.0, 0.0).astype(F32)
    row = lax.broadcasted_iota(jnp.int32, (BLOCK, n), 0)
    lane = lax.broadcasted_iota(jnp.int32, (BLOCK, n), 1)

    def step(j, carry):
        at = pl.ds(pl.multiple_of(j * BLOCK, BLOCK), BLOCK)
        p, v = a_ref[at, :], v_ref[at, :]
        near = pltpu.roll(p, lax.rem(n - j * BLOCK, n), 1)
        cols = [jnp.broadcast_to(near[:, k : k + 1], (BLOCK, n)) for k in range(BLOCK)]
        scale = jnp.zeros((BLOCK, n), F32)
        for k in range(BLOCK):
            pivot = cols[k][k : k + 1, :]
            root = lax.rsqrt(pivot)
            root = root * (1.5 - 0.5 * pivot * root * root)
            mult = jnp.where(row > k, cols[k] * (root * root), 0.0)
            for other in range(k + 1, BLOCK):
                cols[other] = cols[other] - mult * cols[other][k : k + 1, :]
            p = p - mult * p[k : k + 1, :]
            v = v - mult * v[k : k + 1, :]
            scale = jnp.where(row == k, root, scale)
        p, v = p * scale, v * scale
        ahead = jnp.where(lane >= (j + 1) * BLOCK, p, 0.0)
        dims = (((0,), (0,)), ((), ()))
        a_ref[...] -= lax.dot_general(ahead, p, dims, precision=HIGH, preferred_element_type=F32)
        v_ref[...] -= lax.dot_general(ahead, v, dims, precision=HIGH, preferred_element_type=F32)
        v_ref[at, :] = v
        return carry

    lax.fori_loop(0, n // BLOCK, step, 0)


def exchange(
    mom, grad, right, new_right, orth2, cg,
    mom_v, grad_v, b_v, bt_v, rg, pp, prs, pf, gp, gz, gy, gf, inv, cp, cy, cs, cz, own, sq,
    in_sem, r_zs, r_zr, r_ys, r_yr, p_s, p_r, q_s, q_r,
    gz_s, gz_r, gy_s, gy_r, gm_s, gm_r, c_ys, c_yr, c_zs, c_zr, a_zs, a_zr, a_ys, a_yr, s_s, s_r,
):
    M = prs.shape[0]
    rows, cols = b_v.shape
    chunk = cz.shape[1]
    prows = prs.shape[1]
    grows = gz.shape[1]
    f, m = lax.axis_index("fsdp"), lax.axis_index("mat")
    y, z = f // Z, f % Z

    def zpeer(d):
        return (y * Z + lax.rem(z + d, Z), m)

    def ypeer(d):
        return (lax.rem(y + d, Y) * Z + z, m)

    def mpeer(d):
        return (f, lax.rem(m + d, M))

    def part(ref, index, size):
        return ref.at[pl.ds(pl.multiple_of(index * size, size), size)]

    def copy(src, dst, send, recv, device):
        return pltpu.make_async_remote_copy(
            src_ref=src, dst_ref=dst, send_sem=send, recv_sem=recv, device_id=device, device_id_type=MESH
        )

    def loop(lo, hi, body):
        def step(i, carry):
            body(i)
            return carry

        lax.fori_loop(lo, hi, step, 0)

    load_m = pltpu.make_async_copy(mom, mom_v, in_sem.at[0])
    load_g = pltpu.make_async_copy(grad, grad_v, in_sem.at[1])
    load_m.start()
    load_g.start()
    barrier = pltpu.get_barrier_semaphore()
    loop(1, Z, lambda d: pl.semaphore_signal(barrier, 1, device_id=zpeer(d), device_id_type=MESH))
    for d in range(1, Y):
        pl.semaphore_signal(barrier, 1, device_id=ypeer(d), device_id_type=MESH)
    loop(1, M, lambda d: pl.semaphore_signal(barrier, 1, device_id=mpeer(d), device_id_type=MESH))
    part(rg, f, chunk)[...] = right[...].astype(BF16)
    load_m.wait()
    load_g.wait()
    b_v[...] = (mom_v[...].astype(F32) + grad_v[...].astype(F32)).astype(BF16)
    pl.semaphore_wait(barrier, Z - 1 + Y - 1 + M - 1)

    def gather_start(buf, zs, zr, ys, yr):
        mine = part(buf, f, chunk)

        def send(i):
            d = distance(Z - i)
            copy(mine, mine, zs.at[d], zr.at[d], zpeer(d)).start()

        loop(1, Z, send)
        for e in range(1, Y):
            copy(mine, mine, ys.at[e], yr.at[e], ypeer(e)).start()

    def gather_finish(buf, zs, zr, ys, yr):
        def onward(i):
            d = distance(i)
            block = part(buf, y * Z + lax.rem(z - d + Z, Z), chunk)
            copy(block, block, zs.at[d], zr.at[d], zpeer(d)).wait_recv()
            for e in range(1, Y):
                copy(block, block, ys.at[d * Y + e], yr.at[d * Y + e], ypeer(e)).start()

        loop(1, Z, onward)

        def arrive(i):
            d = distance(i) * jnp.minimum(i, 1)
            for e in range(1, Y):
                block = part(buf, lax.rem(y - e + Y, Y) * Z + lax.rem(z - d + Z, Z), chunk)
                copy(block, block, ys.at[d * Y + e], yr.at[d * Y + e], ypeer(e)).wait_recv()

        loop(0, Z, arrive)

    def gather_sent(buf, zs, zr, ys, yr):
        mine = part(buf, f, chunk)
        loop(1, Z, lambda d: copy(mine, mine, zs.at[d], zr.at[d], zpeer(d)).wait_send())

        def sent(d):
            block = part(buf, y * Z + lax.rem(z - d + Z, Z), chunk)
            for e in range(1, Y):
                copy(block, block, ys.at[d * Y + e], yr.at[d * Y + e], ypeer(e)).wait_send()

        loop(0, Z, sent)

    gather_start(rg, r_zs, r_zr, r_ys, r_yr)
    bt_v[...] = b_v[...].T
    gather_finish(rg, r_zs, r_zr, r_ys, r_yr)

    pp[...] = jnp.dot(b_v[...], rg[...], preferred_element_type=F32)
    loop(1, M, lambda d: copy(part(pp, lax.rem(m + d, M), prows), prs.at[d], p_s.at[d], p_r.at[d], mpeer(d)).start())
    prs[0] = part(pp, m, prows)[...]
    loop(1, M, lambda d: copy(part(pp, m, prows), prs.at[d], p_s.at[d], p_r.at[d], mpeer(d)).wait_recv())
    total = prs[0]
    for d in range(1, M):
        total = total + prs[d]
    mine = part(pf, m, prows)
    mine[...] = total
    loop(1, M, lambda d: copy(mine, mine, q_s.at[d], q_r.at[d], mpeer(d)).start())

    def whole(d):
        block = part(pf, lax.rem(m - d + M, M), prows)
        copy(block, block, q_s.at[d], q_r.at[d], mpeer(d)).wait_recv()

    loop(1, M, whole)

    p = pf[...]
    gp[...] = lax.dot_general(p, p, (((0,), (0,)), ((), ())), precision=HIGH, preferred_element_type=F32)
    gmine = part(gp, m, grows)

    def gram_send(i):
        d = distance(Z - i)
        copy(gmine, gz.at[z], gz_s.at[d], gz_r.at[d], zpeer(d)).start()

    loop(1, Z, gram_send)
    gz[z] = gmine[...]

    p1 = p.astype(BF16)
    rest = p - p1.astype(F32)
    p2 = rest.astype(BF16)
    p3 = (rest - p2.astype(F32)).astype(BF16)
    terms = jnp.concatenate([p1, p2, p3], axis=1)
    tile = 512 if cols % 512 == 0 else cols

    def product(i):
        at = pl.ds(pl.multiple_of(i * tile, tile), tile)
        out = jnp.dot(bt_v[at, :], terms, preferred_element_type=F32)
        cp[at, :] = out[:, :RANK] + out[:, RANK : 2 * RANK] + out[:, 2 * RANK :]

    loop(0, cols // tile, product)

    def target(i):
        i = Z - 1 - i
        return distance(i) * jnp.minimum(i, 1)

    def spread(i):
        d = target(i)
        to = lax.rem(z + d, Z)
        for e in range(1, Y):
            block = part(cp, lax.rem(y + e, Y) * Z + to, chunk)
            copy(block, cy.at[d * Y + e], c_ys.at[d * Y + e], c_yr.at[d * Y + e], ypeer(e)).start()

    loop(0, Z, spread)

    def combine(i):
        d = target(i)
        block = part(cp, y * Z + lax.rem(z + d, Z), chunk)
        for e in range(1, Y):
            copy(block, cy.at[d * Y + e], c_ys.at[d * Y + e], c_yr.at[d * Y + e], ypeer(e)).wait_recv()
        out = block[...]
        for e in range(1, Y):
            out = out + cy[d * Y + e]
        cs[d] = out

    def combine_send(i):
        combine(i)
        d = target(i)
        copy(cs.at[d], cz.at[d], c_zs.at[d], c_zr.at[d], zpeer(d)).start()

    loop(0, Z // 2, combine_send)

    def gram_arrive(d):
        slot = gz.at[lax.rem(z - d + Z, Z)]
        copy(gmine, slot, gz_s.at[d], gz_r.at[d], zpeer(d)).wait_recv()

    loop(1, Z, gram_arrive)
    total = gz[0]
    for k in range(1, Z):
        total = total + gz[k]
    gy[y] = total
    for e in range(1, Y):
        copy(gy.at[y], gy.at[y], gy_s.at[e], gy_r.at[e], ypeer(e)).start()

    loop(Z // 2, Z - 1, combine_send)
    combine(Z - 1)

    for e in range(1, Y):
        slot = gy.at[lax.rem(y - e + Y, Y)]
        copy(slot, slot, gy_s.at[e], gy_r.at[e], ypeer(e)).wait_recv()
    total = gy[0]
    for k in range(1, Y):
        total = total + gy[k]
    gown = part(gf, m, grows)
    gown[...] = total
    loop(1, M, lambda d: copy(gown, gown, gm_s.at[d], gm_r.at[d], mpeer(d)).start())

    def gram_whole(d):
        block = part(gf, lax.rem(m - d + M, M), grows)
        copy(block, block, gm_s.at[d], gm_r.at[d], mpeer(d)).wait_recv()

    loop(1, M, gram_whole)
    loop(1, M, lambda d: copy(gown, gown, gm_s.at[d], gm_r.at[d], mpeer(d)).wait_send())

    factor_inverse(gf, inv)
    nt = (((1,), (1,)), ((), ()))
    linv = inv[...]

    total = cs[0]
    for d in range(1, Z):
        copy(cs.at[d], cz.at[d], c_zs.at[d], c_zr.at[d], zpeer(d)).wait_recv()
        total = total + cz[d]
    columns = lax.dot_general(total, linv, nt, precision=HIGH, preferred_element_type=F32)
    own[...] = columns
    part(cg, f, chunk)[...] = columns.astype(BF16)
    gather_start(cg, a_zs, a_zr, a_ys, a_yr)
    orth = lax.dot_general(pf[...], linv, nt, precision=HIGH, preferred_element_type=F32).astype(BF16)
    orth2[pl.ds(0, rows), :] = orth
    gather_finish(cg, a_zs, a_zr, a_ys, a_yr)

    here = cg[...].astype(F32)
    sq[m] = jnp.broadcast_to(jnp.sum(here * here, axis=0, keepdims=True), sq.shape[1:])
    loop(1, M, lambda d: copy(sq.at[m], sq.at[m], s_s.at[d], s_r.at[d], mpeer(d)).start())

    def squares(d):
        slot = sq.at[lax.rem(m - d + M, M)]
        copy(slot, slot, s_s.at[d], s_r.at[d], mpeer(d)).wait_recv()

    loop(1, M, squares)
    total = sq[0]
    for k in range(1, M):
        total = total + sq[k]
    scale = math.sqrt(D) * lax.rsqrt(total[0:1, :] + norm_eps)
    new_right[...] = own[...] * scale
    orth2[pl.ds(rows, rows), :] = (orth.astype(F32) * (math.sqrt(D / RANK) * scale)).astype(BF16)

    gather_sent(rg, r_zs, r_zr, r_ys, r_yr)
    gather_sent(cg, a_zs, a_zr, a_ys, a_yr)
    loop(1, M, lambda d: copy(part(pp, m, prows), prs.at[d], p_s.at[d], p_r.at[d], mpeer(d)).wait_send())
    loop(1, M, lambda d: copy(mine, mine, q_s.at[d], q_r.at[d], mpeer(d)).wait_send())
    loop(1, Z, lambda d: copy(gmine, gz.at[z], gz_s.at[d], gz_r.at[d], zpeer(d)).wait_send())
    for e in range(1, Y):
        copy(gy.at[y], gy.at[y], gy_s.at[e], gy_r.at[e], ypeer(e)).wait_send()

    def spread_sent(d):
        for e in range(1, Y):
            copy(cs.at[d], cy.at[d * Y + e], c_ys.at[d * Y + e], c_yr.at[d * Y + e], ypeer(e)).wait_send()

    loop(0, Z, spread_sent)
    loop(1, Z, lambda d: copy(cs.at[d], cz.at[d], c_zs.at[d], c_zr.at[d], zpeer(d)).wait_send())
    loop(1, M, lambda d: copy(sq.at[m], sq.at[m], s_s.at[d], s_r.at[d], mpeer(d)).wait_send())


def finish(mom, grad, orth2, columns, new_momentum, update):
    rows = mom.shape[0]
    buffer = (mom[...].astype(F32) + grad[...].astype(F32)).astype(BF16).astype(F32)
    both = lax.dot_general(orth2[...], columns[...], (((1,), (1,)), ((), ())), preferred_element_type=F32)
    new_momentum[...] = (buffer - (1.0 - keep_factor) * both[:rows]).astype(BF16)
    update[...] = both[rows:].astype(BF16)


def local(momentum, gradient, right_factor):
    rows, cols = momentum.shape
    chunk = right_factor.shape[0]
    F, M = lax.axis_size("fsdp"), lax.axis_size("mat")
    prows, grows = rows // M, RANK // M
    vmem, dma = pltpu.VMEM, pltpu.SemaphoreType.DMA
    whole = pl.BlockSpec(memory_space=pltpu.VMEM)
    anyw = pl.BlockSpec(memory_space=pl.ANY)
    ring = [dma((Z,)), dma((Z,))]
    plane = [dma((Z * Y,)), dma((Z * Y,))]
    pair = [dma((M,)), dma((M,))]
    new_right, orth2, columns = pl.pallas_call(
        exchange,
        out_shape=(
            jax.ShapeDtypeStruct((chunk, RANK), F32),
            jax.ShapeDtypeStruct((2 * rows, RANK), BF16),
            jax.ShapeDtypeStruct((cols, RANK), BF16),
        ),
        in_specs=[anyw, anyw, whole],
        out_specs=(whole, whole, whole),
        scratch_shapes=[
            vmem((rows, cols), BF16), vmem((rows, cols), BF16), vmem((rows, cols), BF16), vmem((cols, rows), BF16),
            vmem((cols, RANK), BF16), vmem((rows, RANK), F32), vmem((M, prows, RANK), F32), vmem((rows, RANK), F32),
            vmem((RANK, RANK), F32), vmem((Z, grows, RANK), F32), vmem((Y, grows, RANK), F32),
            vmem((RANK, RANK), F32), vmem((RANK, RANK), F32),
            vmem((cols, RANK), F32), vmem((Z * Y, chunk, RANK), F32), vmem((Z, chunk, RANK), F32),
            vmem((Z, chunk, RANK), F32), vmem((chunk, RANK), F32), vmem((M, 8, RANK), F32),
            dma((2,)), *ring, *plane, *pair, *pair, *ring, dma((Y,)), dma((Y,)), *pair, *plane, *ring, *ring, *plane, *pair,
        ],
        compiler_params=pltpu.CompilerParams(
            collective_id=0, has_side_effects=True, vmem_limit_bytes=40 * 2**20
        ),
        name="exchange",
    )(momentum, gradient, right_factor)
    tile = min(512, cols)
    wide = pl.BlockSpec((rows, tile), lambda i: (0, i))
    new_momentum, update = pl.pallas_call(
        finish,
        grid=(cols // tile,),
        out_shape=(
            jax.ShapeDtypeStruct((rows, cols), BF16),
            jax.ShapeDtypeStruct((rows, cols), BF16),
        ),
        in_specs=[wide, wide, pl.BlockSpec((2 * rows, RANK), lambda i: (0, 0)), pl.BlockSpec((tile, RANK), lambda i: (i, 0))],
        out_specs=(wide, wide),
        name="finish",
    )(momentum, gradient, orth2, columns)
    return (new_momentum, update, new_right)


def solution(mesh):
    placed = (P("fsdp", "mat"), P("fsdp", "mat"), P(("mat", "fsdp"), None))
    return jax.shard_map(
        local,
        mesh=mesh,
        in_specs=placed,
        out_specs=(P("fsdp", "mat"), P("fsdp", "mat"), P(("mat", "fsdp"), None)),
        check_vma=False,
    )
```

```python
import functools
import math

import jax
import jax.numpy as jnp
from jax import lax
from jax.experimental import pallas as pl
from jax.experimental.pallas import tpu as pltpu
from jax.sharding import PartitionSpec as P

D = 16384
RANK = 128
Y, Z = 4, 16

keep_factor = 0.95
norm_eps = 1e-06

MESH = pl.DeviceIdType.MESH
F32, BF16 = jnp.float32, jnp.bfloat16
HIGH = lax.Precision.HIGHEST
BLOCK = 32
EARLY = 5


def factor_inverse(a_ref, v_ref):
    n = a_ref.shape[0]
    rows = lax.broadcasted_iota(jnp.int32, (n, n), 0)
    lanes = lax.broadcasted_iota(jnp.int32, (n, n), 1)
    v_ref[...] = jnp.where(rows == lanes, 1.0, 0.0).astype(F32)
    row = lax.broadcasted_iota(jnp.int32, (BLOCK, n), 0)
    lane = lax.broadcasted_iota(jnp.int32, (BLOCK, n), 1)

    def step(j, carry):
        at = pl.ds(pl.multiple_of(j * BLOCK, BLOCK), BLOCK)
        p, v = a_ref[at, :], v_ref[at, :]
        near = pltpu.roll(p, lax.rem(n - j * BLOCK, n), 1)
        cols = [jnp.broadcast_to(near[:, k : k + 1], (BLOCK, n)) for k in range(BLOCK)]
        scale = jnp.zeros((BLOCK, n), F32)
        for k in range(BLOCK):
            pivot = cols[k][k : k + 1, :]
            root = lax.rsqrt(pivot)
            root = root * (1.5 - 0.5 * pivot * root * root)
            mult = jnp.where(row > k, cols[k] * (root * root), 0.0)
            for other in range(k + 1, BLOCK):
                cols[other] = cols[other] - mult * cols[other][k : k + 1, :]
            p = p - mult * p[k : k + 1, :]
            v = v - mult * v[k : k + 1, :]
            scale = jnp.where(row == k, root, scale)
        p, v = p * scale, v * scale
        ahead = jnp.where(lane >= (j + 1) * BLOCK, p, 0.0)
        dims = (((0,), (0,)), ((), ()))
        a_ref[...] -= lax.dot_general(ahead, p, dims, precision=HIGH, preferred_element_type=F32)
        v_ref[...] -= lax.dot_general(ahead, v, dims, precision=HIGH, preferred_element_type=F32)
        v_ref[at, :] = v
        return carry

    lax.fori_loop(0, n // BLOCK, step, 0)


def exchange(
    mom, grad, right, new_right, new_momentum, update,
    mom_v, grad_v, right_v, cg, b_v, bt_v, rg, pp, prs, pf, gp, gy, gz, gf, inv, orth_v, cp, cy, cs, cz, own, sm, sy,
    in_sem, p_s, p_r, q_s, q_r, gy_s, gy_r, gz_s, gz_r, gm_s, gm_r, cy_s, cy_r, cz_s, cz_r,
    sm_s, sm_r, sy_s, sy_r, rz_s, rz_r, ry_s, ry_r, az_s, az_r, ay_s, ay_r,
):
    M = prs.shape[0]
    rows, cols = b_v.shape
    chunk = cz.shape[1]
    prows = prs.shape[1]
    grows = gz.shape[1]
    F = Y * Z
    tile = cols // Y
    ring = [d for k in range(1, Z // 2) for d in (k, Z - k)] + [Z // 2]
    nt = (((1,), (1,)), ((), ()))
    f, m = lax.axis_index("fsdp"), lax.axis_index("mat")
    y, z = f // Z, f % Z

    def zpeer(d):
        return (y * Z + lax.rem(z + d, Z), m)

    def ypeer(d):
        return (lax.rem(y + d, Y) * Z + z, m)

    def mpeer(d):
        return (f, lax.rem(m + d, M))

    def part(ref, index, size):
        return ref.at[pl.ds(pl.multiple_of(index * size, size), size)]

    def copy(src, dst, send, recv, device):
        return pltpu.make_async_remote_copy(
            src_ref=src, dst_ref=dst, send_sem=send, recv_sem=recv, device_id=device, device_id_type=MESH
        )

    def arrived(ref, sem):
        copy(ref, ref, sem, sem, zpeer(1)).wait_recv()

    pending = []

    def sent(ref, sem):
        pending.append(lambda: copy(ref, ref, sem, sem, zpeer(1)).wait_send())

    barrier = pltpu.get_barrier_semaphore()
    peers = [zpeer(d) for d in reversed(ring)] + [mpeer(d) for d in range(1, M)] + [ypeer(d) for d in range(1, Y)]
    for peer in peers:
        pl.semaphore_signal(barrier, 1, device_id=peer, device_id_type=MESH)
    load_m = pltpu.make_async_copy(mom, mom_v, in_sem.at[0])
    load_g = pltpu.make_async_copy(grad, grad_v, in_sem.at[1])
    load_r = pltpu.make_async_copy(right, right_v, in_sem.at[2])
    load_r.start()
    load_m.start()
    load_g.start()
    load_r.wait()
    part(rg, f, chunk)[...] = right_v[...].astype(BF16)
    load_m.wait()
    load_g.wait()
    b_v[...] = (mom_v[...].astype(F32) + grad_v[...].astype(F32)).astype(BF16)
    pl.semaphore_wait(barrier, len(peers))

    def block_of(buf, d):
        return part(buf, y * Z + lax.rem(z - d + Z, Z), chunk)

    def along_y(buf, d, y_s, y_r):
        block = block_of(buf, d)
        for e in (2, 1, 3):
            copy(block, block, y_s, y_r, ypeer(e)).start()

    def gather_z(buf, z_s, z_r, y_s, y_r, beside):
        mine = block_of(buf, 0)
        far = [d for d in ring if Z // 4 < d < Z - Z // 4]
        for d in reversed(far):
            copy(mine, mine, z_s, z_r.at[d], zpeer(d)).start()
        along_y(buf, 0, y_s, y_r)
        for d in ring:
            if d not in far:
                copy(mine, mine, z_s, z_r.at[d], zpeer(d)).start()
        beside()
        for d in ring:
            arrived(block_of(buf, d), z_r.at[d])
            along_y(buf, d, y_s, y_r)
        sent(buf.at[pl.ds(0, (Z - 1) * chunk)], z_s)
        sent(buf.at[pl.ds(0, (F - Z) * chunk)], y_s)

    def gather_y(buf, y_r):
        arrived(buf.at[pl.ds(0, (F - Z) * chunk)], y_r)

    def turned():
        bt_v[...] = b_v[...].T

    gather_z(rg, rz_s, rz_r, ry_s, ry_r, turned)
    gather_y(rg, ry_r)

    pp[...] = jnp.dot(b_v[...], rg[...], preferred_element_type=F32)
    for d in range(1, M):
        copy(part(pp, lax.rem(m + d, M), prows), prs.at[d], p_s, p_r, mpeer(d)).start()
    prs[0] = part(pp, m, prows)[...]
    arrived(prs.at[pl.ds(1, M - 1)], p_r)
    sent(prs.at[pl.ds(1, M - 1)], p_s)
    total = prs[0]
    for d in range(1, M):
        total = total + prs[d]
    mine = part(pf, m, prows)
    mine[...] = total
    for d in range(1, M):
        copy(mine, mine, q_s, q_r, mpeer(d)).start()
    arrived(pf.at[pl.ds(0, (M - 1) * prows)], q_r)
    sent(pf.at[pl.ds(0, (M - 1) * prows)], q_s)

    p = pf[...]
    gp[...] = lax.dot_general(p, p, (((0,), (0,)), ((), ())), precision=HIGH, preferred_element_type=F32)
    gmine = part(gp, m, grows)

    gy[y] = gmine[...]
    for e in (2, 1, 3):
        copy(gmine, gy.at[y], gy_s, gy_r, ypeer(e)).start()
    sent(gy.at[pl.ds(0, Y - 1)], gy_s)

    p1 = p.astype(BF16)
    rest = p - p1.astype(F32)
    p2 = rest.astype(BF16)
    p3 = (rest - p2.astype(F32)).astype(BF16)
    terms = jnp.concatenate([p1, p2, p3], axis=1)
    def product(i):
        at = pl.ds(pl.multiple_of(i * tile, tile), tile)
        out = jnp.dot(bt_v[at, :], terms, preferred_element_type=F32)
        cp[at, :] = out[:, :RANK] + out[:, RANK : 2 * RANK] + out[:, 2 * RANK :]

    def loop(lo, hi, body):
        def step(i, carry):
            body(i)
            return carry

        lax.fori_loop(lo, hi, step, 0)

    loop(0, Y, product)

    def term(e, d):
        return part(cp, lax.rem(y + e, Y) * Z + lax.rem(z + d, Z), chunk)

    order = [*reversed(ring), 0]
    for d in order:
        for e in (2, 1, 3):
            copy(term(e, d), cy.at[d, e - 1], cy_s, cy_r.at[d], ypeer(e)).start()
    sent(cp.at[pl.ds(0, (F - Z) * chunk)], cy_s)

    arrived(gy.at[pl.ds(0, Y - 1)], gy_r)
    total = gy[0]
    for k in range(1, Y):
        total = total + gy[k]
    gz[z] = total
    for d in reversed(ring):
        copy(gz.at[z], gz.at[z], gz_s, gz_r, zpeer(d)).start()
    sent(gz.at[pl.ds(0, Z - 1)], gz_s)

    def combine(d):
        arrived(cy.at[d], cy_r.at[d])
        cs[d] = term(0, d)[...] + cy[d, 0] + cy[d, 1] + cy[d, 2]

    def combine_send(d):
        combine(d)
        copy(cs.at[d], cz.at[d], cz_s, cz_r, zpeer(d)).start()

    for d in order[:EARLY]:
        combine_send(d)

    arrived(gz.at[pl.ds(0, Z - 1)], gz_r)
    total = gz[0]
    for k in range(1, Z):
        total = total + gz[k]
    gown = part(gf, m, grows)
    gown[...] = total
    for d in range(1, M):
        copy(gown, gown, gm_s, gm_r, mpeer(d)).start()
    for d in order[EARLY : Z - 1]:
        combine_send(d)
    combine(0)
    arrived(gf.at[pl.ds(0, (M - 1) * grows)], gm_r)
    copy(gf.at[pl.ds(0, (M - 1) * grows)], gown, gm_s, gm_s, zpeer(1)).wait_send()

    factor_inverse(gf, inv)
    sent(cz.at[pl.ds(0, Z - 1)], cz_s)
    linv = inv[...]

    arrived(cz.at[pl.ds(1, Z - 1)], cz_r)
    total = cs[0]
    for d in range(1, Z):
        total = total + cz[d]
    columns = lax.dot_general(total, linv, nt, precision=HIGH, preferred_element_type=F32)
    own[...] = columns
    part(cg, f, chunk)[...] = columns.astype(BF16)

    def turned_back():
        orth_v[...] = lax.dot_general(pf[...], linv, nt, precision=HIGH, preferred_element_type=F32).astype(BF16)

    gather_z(cg, az_s, az_r, ay_s, ay_r, turned_back)

    here = part(cg, y, tile)[...].astype(F32)
    sm[m] = jnp.sum(here * here, axis=0, keepdims=True)
    for d in range(1, M):
        copy(sm.at[m], sm.at[m], sm_s, sm_r, mpeer(d)).start()
    sent(sm.at[pl.ds(0, M - 1)], sm_s)

    def feedback(i):
        at = pl.ds(pl.multiple_of(i * tile, tile), tile)
        out = lax.dot_general(orth_v[...], cg[at, :], nt, preferred_element_type=F32)
        new_momentum[:, at] = (b_v[:, at].astype(F32) - (1.0 - keep_factor) * out).astype(BF16)

    feedback(y)
    arrived(sm.at[pl.ds(0, M - 1)], sm_r)
    total = sm[0]
    for k in range(1, M):
        total = total + sm[k]
    sy[y] = total
    for e in (2, 1, 3):
        copy(sy.at[y], sy.at[y], sy_s, sy_r, ypeer(e)).start()
    sent(sy.at[pl.ds(0, Y - 1)], sy_s)
    gather_y(cg, ay_r)
    loop(1, Y, lambda e: feedback(lax.rem(y + e, Y)))
    arrived(sy.at[pl.ds(0, Y - 1)], sy_r)
    total = sy[0]
    for k in range(1, Y):
        total = total + sy[k]
    scale = math.sqrt(D) * lax.rsqrt(total + norm_eps)
    new_right[...] = own[...] * scale
    scaled = (orth_v[...].astype(F32) * (math.sqrt(D / RANK) * scale)).astype(BF16)

    def outer(i):
        at = pl.ds(pl.multiple_of(i * tile, tile), tile)
        update[:, at] = lax.dot_general(scaled, cg[at, :], nt, preferred_element_type=F32).astype(BF16)

    loop(0, Y, outer)

    for wait in pending:
        wait()


def local(momentum, gradient, right_factor):
    rows, cols = momentum.shape
    chunk = right_factor.shape[0]
    F, M = lax.axis_size("fsdp"), lax.axis_size("mat")
    prows, grows = rows // M, RANK // M
    vmem, dma = pltpu.VMEM, pltpu.SemaphoreType.DMA
    whole = pl.BlockSpec(memory_space=pltpu.VMEM)
    hbm = pl.BlockSpec(memory_space=pltpu.HBM)
    ring = [dma((Z,)), dma((Z,))]
    plane = [dma((Z * Y,)), dma((Z * Y,))]
    pair = [dma((M,)), dma((M,))]
    new_right, new_momentum, update = pl.pallas_call(
        exchange,
        out_shape=(
            jax.ShapeDtypeStruct((chunk, RANK), F32),
            jax.ShapeDtypeStruct((rows, cols), BF16),
            jax.ShapeDtypeStruct((rows, cols), BF16),
        ),
        in_specs=[hbm, hbm, hbm],
        out_specs=(whole, whole, whole),
        scratch_shapes=[
            vmem((rows, cols), BF16), vmem((rows, cols), BF16), vmem((chunk, RANK), F32), vmem((cols, RANK), BF16),
            vmem((rows, cols), BF16), vmem((cols, rows), BF16),
            vmem((cols, RANK), BF16), vmem((rows, RANK), F32), vmem((M, prows, RANK), F32), vmem((rows, RANK), F32),
            vmem((RANK, RANK), F32), vmem((Y, grows, RANK), F32), vmem((Z, grows, RANK), F32),
            vmem((RANK, RANK), F32), vmem((RANK, RANK), F32), vmem((rows, RANK), BF16),
            vmem((cols, RANK), F32), vmem((Z, Y - 1, chunk, RANK), F32), vmem((Z, chunk, RANK), F32),
            vmem((Z, chunk, RANK), F32), vmem((chunk, RANK), F32), vmem((M, 1, RANK), F32), vmem((Y, 1, RANK), F32),
            dma((3,)), *[dma(())] * 11, dma((Z,)), *[dma(())] * 6, *[dma(()), dma((Z,)), dma(()), dma(())] * 2,
        ],
        compiler_params=pltpu.CompilerParams(
            collective_id=0, has_side_effects=True, vmem_limit_bytes=51 * 2**20
        ),
        name="exchange",
    )(momentum, gradient, right_factor)
    return (new_momentum, update, new_right)


def solution(mesh):
    placed = (P("fsdp", "mat"), P("fsdp", "mat"), P(("mat", "fsdp"), None))
    return jax.shard_map(
        local,
        mesh=mesh,
        in_specs=placed,
        out_specs=(P("fsdp", "mat"), P("fsdp", "mat"), P(("mat", "fsdp"), None)),
        check_vma=False,
    )
```

```python
import functools
import math

import jax
import jax.numpy as jnp
from jax import lax
from jax.experimental import pallas as pl
from jax.experimental.pallas import tpu as pltpu
from jax.sharding import PartitionSpec as P

D = 16384
RANK = 128
Y, Z = 4, 16

keep_factor = 0.95
norm_eps = 1e-06

MESH = pl.DeviceIdType.MESH
F32, BF16 = jnp.float32, jnp.bfloat16
HIGH = lax.Precision.HIGHEST
BLOCK = 32
EARLY = 5


def factor_inverse(a_ref, v_ref):
    n = a_ref.shape[0]
    rows = lax.broadcasted_iota(jnp.int32, (n, n), 0)
    lanes = lax.broadcasted_iota(jnp.int32, (n, n), 1)
    v_ref[...] = jnp.where(rows == lanes, 1.0, 0.0).astype(F32)
    row = lax.broadcasted_iota(jnp.int32, (BLOCK, n), 0)
    lane = lax.broadcasted_iota(jnp.int32, (BLOCK, n), 1)

    def step(j, carry):
        at = pl.ds(pl.multiple_of(j * BLOCK, BLOCK), BLOCK)
        p, v = a_ref[at, :], v_ref[at, :]
        near = pltpu.roll(p, lax.rem(n - j * BLOCK, n), 1)
        cols = [jnp.broadcast_to(near[:, k : k + 1], (BLOCK, n)) for k in range(BLOCK)]
        pivots = jnp.zeros((BLOCK, n), F32)
        for k in range(BLOCK):
            pivot = cols[k][k : k + 1, :]
            root = lax.rsqrt(pivot)
            root = root * (1.5 - 0.5 * pivot * root * root)
            mult = jnp.where(row > k, cols[k] * (root * root), 0.0)
            for other in range(k + 1, BLOCK):
                cols[other] = cols[other] - mult * cols[other][k : k + 1, :]
            p = p - mult * p[k : k + 1, :]
            v = v - mult * v[k : k + 1, :]
            pivots = jnp.where(row == k, pivot, pivots)
        scale = lax.rsqrt(pivots)
        scale = scale * (1.5 - 0.5 * pivots * scale * scale)
        p, v = p * scale, v * scale
        ahead = jnp.where(lane >= (j + 1) * BLOCK, p, 0.0)
        dims = (((0,), (0,)), ((), ()))
        a_ref[...] -= lax.dot_general(ahead, p, dims, precision=HIGH, preferred_element_type=F32)
        v_ref[...] -= lax.dot_general(ahead, v, dims, precision=HIGH, preferred_element_type=F32)
        v_ref[at, :] = v
        return carry

    lax.fori_loop(0, n // BLOCK, step, 0)


def exchange(
    mom, grad, right, new_right, new_momentum, update,
    mom_v, grad_v, right_v, cg, b_v, bt_v, rg, pp, prs, pf, gp, gy, gz, gf, inv, orth_v, cp, cy, cs, cz, own, sm, sz, sy,
    in_sem, p_s, p_r, q_s, q_r, gy_s, gy_r, gz_s, gz_r, gm_s, gm_r, cy_s, cy_r, cz_s, cz_r,
    sm_s, sm_r, sz_s, sz_r, sy_s, sy_r, rz_s, rz_r, ry_s, ry_r, az_s, az_r, ay_s, ay_r,
):
    M = prs.shape[0]
    rows, cols = b_v.shape
    chunk = cz.shape[1]
    prows = prs.shape[1]
    grows = gz.shape[1]
    F = Y * Z
    tile = cols // Y
    ring = [d for k in range(1, Z // 2) for d in (k, Z - k)] + [Z // 2]
    mats = sorted(range(1, M), key=lambda d: abs(2 * d - M))
    nt = (((1,), (1,)), ((), ()))
    f, m = lax.axis_index("fsdp"), lax.axis_index("mat")
    y, z = f // Z, f % Z

    def zpeer(d):
        return (y * Z + lax.rem(z + d, Z), m)

    def ypeer(d):
        return (lax.rem(y + d, Y) * Z + z, m)

    def mpeer(d):
        return (f, lax.rem(m + d, M))

    def part(ref, index, size):
        return ref.at[pl.ds(pl.multiple_of(index * size, size), size)]

    def copy(src, dst, send, recv, device):
        return pltpu.make_async_remote_copy(
            src_ref=src, dst_ref=dst, send_sem=send, recv_sem=recv, device_id=device, device_id_type=MESH
        )

    def arrived(ref, sem):
        copy(ref, ref, sem, sem, zpeer(1)).wait_recv()

    pending = []

    def sent(ref, sem):
        pending.append(lambda: copy(ref, ref, sem, sem, zpeer(1)).wait_send())

    barrier = pltpu.get_barrier_semaphore()
    near = Z // 4
    peers = [zpeer(d) for d in reversed(ring[: 2 * near])] + [mpeer(d) for d in range(1, M)] + [ypeer(d) for d in range(1, Y)]
    for peer in peers:
        pl.semaphore_signal(barrier, 1, device_id=peer, device_id_type=MESH)
    load_m = pltpu.make_async_copy(mom, mom_v, in_sem.at[0])
    load_g = pltpu.make_async_copy(grad, grad_v, in_sem.at[1])
    load_r = pltpu.make_async_copy(right, right_v, in_sem.at[2])
    load_r.start()
    load_m.start()
    load_g.start()
    load_r.wait()
    part(rg, f, chunk)[...] = right_v[...].astype(BF16)
    load_m.wait()
    load_g.wait()
    b_v[...] = (mom_v[...].astype(F32) + grad_v[...].astype(F32)).astype(BF16)
    pl.semaphore_wait(barrier, len(peers))

    def block_of(buf, d):
        return part(buf, y * Z + lax.rem(z - d + Z, Z), chunk)

    def along_y(buf, d, y_s, y_r):
        block = block_of(buf, d)
        for e in (2, 1, 3):
            copy(block, block, y_s, y_r.at[e], ypeer(e)).start()

    def gather_z(buf, z_s, z_r, y_s, y_r, beside):
        mine = block_of(buf, 0)
        far = [d for d in ring if Z // 4 < d < Z - Z // 4]
        for d in reversed(far):
            copy(mine, mine, z_s, z_r.at[d], zpeer(d)).start()
        along_y(buf, 0, y_s, y_r)
        for d in ring:
            if d not in far:
                copy(mine, mine, z_s, z_r.at[d], zpeer(d)).start()
        beside()
        for d in ring:
            arrived(block_of(buf, d), z_r.at[d])
            along_y(buf, d, y_s, y_r)
        sent(buf.at[pl.ds(0, (Z - 1) * chunk)], z_s)
        sent(buf.at[pl.ds(0, (F - Z) * chunk)], y_s)

    def gather_z_relayed(buf, z_s, z_r, y_s, y_r, beside):
        def along_z(d, k):
            to = (d + k) % Z
            copy(block_of(buf, d), block_of(buf, d), z_s, z_r.at[to], zpeer(k)).start()

        def take(d):
            arrived(block_of(buf, d), z_r.at[d])

        for k in range(near, 0, -1):
            along_z(0, k)
            along_z(0, Z - k)
        along_y(buf, 0, y_s, y_r)
        beside()
        first = ring[: near // 2 * 2]
        for d in first:
            take(d)
            along_y(buf, d, y_s, y_r)
        take(near)
        for k in range(near, 0, -1):
            along_z(near, k)
        take(Z - near)
        for k in range(near - 1, 0, -1):
            along_z(Z - near, Z - k)
        along_y(buf, near, y_s, y_r)
        along_y(buf, Z - near, y_s, y_r)
        for d in ring:
            if d not in (*first, near, Z - near):
                take(d)
                along_y(buf, d, y_s, y_r)
        sent(buf.at[pl.ds(0, (Z - 1) * chunk)], z_s)
        sent(buf.at[pl.ds(0, (F - Z) * chunk)], y_s)

    def gather_y(buf, y_r, e):
        arrived(buf.at[pl.ds(0, Z * chunk)], y_r.at[e])

    def turned():
        bt_v[...] = b_v[...].T

    gather_z_relayed(rg, rz_s, rz_r, ry_s, ry_r, turned)

    for e in (1, 3, 2):
        gather_y(rg, ry_r, e)
    pp[...] = jnp.dot(b_v[...], rg[...], preferred_element_type=F32)
    for d in mats:
        copy(part(pp, lax.rem(m + d, M), prows), prs.at[d], p_s, p_r, mpeer(d)).start()
    prs[0] = part(pp, m, prows)[...]
    arrived(prs.at[pl.ds(1, M - 1)], p_r)
    sent(prs.at[pl.ds(1, M - 1)], p_s)
    total = prs[0]
    for d in range(1, M):
        total = total + prs[d]
    mine = part(pf, m, prows)
    mine[...] = total
    for d in mats:
        copy(mine, mine, q_s, q_r, mpeer(d)).start()
    arrived(pf.at[pl.ds(0, (M - 1) * prows)], q_r)
    sent(pf.at[pl.ds(0, (M - 1) * prows)], q_s)

    p = pf[...]
    gp[...] = lax.dot_general(p, p, (((0,), (0,)), ((), ())), precision=HIGH, preferred_element_type=F32)
    gmine = part(gp, m, grows)

    gy[y] = gmine[...]
    for e in (2, 1, 3):
        copy(gmine, gy.at[y], gy_s, gy_r, ypeer(e)).start()
    sent(gy.at[pl.ds(0, Y - 1)], gy_s)

    p1 = p.astype(BF16)
    rest = p - p1.astype(F32)
    p2 = rest.astype(BF16)
    p3 = (rest - p2.astype(F32)).astype(BF16)
    terms = jnp.concatenate([p1, p2, p3], axis=1)
    def product(i):
        at = pl.ds(pl.multiple_of(i * tile, tile), tile)
        out = jnp.dot(bt_v[at, :], terms, preferred_element_type=F32)
        cp[at, :] = out[:, :RANK] + out[:, RANK : 2 * RANK] + out[:, 2 * RANK :]

    def loop(lo, hi, body):
        def step(i, carry):
            body(i)
            return carry

        lax.fori_loop(lo, hi, step, 0)

    loop(0, Y, product)

    def term(e, d):
        return part(cp, lax.rem(y + e, Y) * Z + lax.rem(z + d, Z), chunk)

    order = [*reversed(ring), 0]
    for d in order:
        for e in (2, 1, 3):
            copy(term(e, d), cy.at[d, e - 1], cy_s, cy_r.at[d], ypeer(e)).start()
    sent(cp.at[pl.ds(0, (F - Z) * chunk)], cy_s)

    arrived(gy.at[pl.ds(0, Y - 1)], gy_r)
    total = gy[0]
    for k in range(1, Y):
        total = total + gy[k]
    gz[z] = total
    for d in reversed(ring):
        copy(gz.at[z], gz.at[z], gz_s, gz_r, zpeer(d)).start()
    sent(gz.at[pl.ds(0, Z - 1)], gz_s)

    def combine(d):
        arrived(cy.at[d], cy_r.at[d])
        cs[d] = term(0, d)[...] + cy[d, 0] + cy[d, 1] + cy[d, 2]

    def combine_send(d):
        combine(d)
        copy(cs.at[d], cz.at[d], cz_s, cz_r, zpeer(d)).start()

    for d in order[:EARLY]:
        combine_send(d)

    arrived(gz.at[pl.ds(0, Z - 1)], gz_r)
    total = gz[0]
    for k in range(1, Z):
        total = total + gz[k]
    gown = part(gf, m, grows)
    gown[...] = total
    for d in mats:
        copy(gown, gown, gm_s, gm_r, mpeer(d)).start()
    for d in order[EARLY : Z - 1]:
        combine_send(d)
    combine(0)
    arrived(gf.at[pl.ds(0, (M - 1) * grows)], gm_r)
    copy(gf.at[pl.ds(0, (M - 1) * grows)], gown, gm_s, gm_s, zpeer(1)).wait_send()

    factor_inverse(gf, inv)
    sent(cz.at[pl.ds(0, Z - 1)], cz_s)
    linv = inv[...]

    arrived(cz.at[pl.ds(1, Z - 1)], cz_r)
    total = cs[0]
    for d in range(1, Z):
        total = total + cz[d]
    columns = lax.dot_general(total, linv, nt, precision=HIGH, preferred_element_type=F32)
    own[...] = columns
    part(cg, f, chunk)[...] = columns.astype(BF16)

    sm[m] = jnp.sum(columns * columns, axis=0, keepdims=True)

    def squares():
        for d in mats:
            copy(sm.at[m], sm.at[m], sm_s, sm_r, mpeer(d)).start()
        sent(sm.at[pl.ds(0, M - 1)], sm_s)
        orth_v[...] = lax.dot_general(pf[...], linv, nt, precision=HIGH, preferred_element_type=F32).astype(BF16)
        arrived(sm.at[pl.ds(0, M - 1)], sm_r)
        total = sm[0]
        for k in range(1, M):
            total = total + sm[k]
        sz[z] = total
        for d in reversed(ring):
            copy(sz.at[z], sz.at[z], sz_s, sz_r, zpeer(d)).start()
        sent(sz.at[pl.ds(0, Z - 1)], sz_s)

    gather_z(cg, az_s, az_r, ay_s, ay_r, squares)
    arrived(sz.at[pl.ds(0, Z - 1)], sz_r)
    total = sz[0]
    for k in range(1, Z):
        total = total + sz[k]
    sy[y] = total
    for e in (2, 1, 3):
        copy(sy.at[y], sy.at[y], sy_s, sy_r, ypeer(e)).start()
    sent(sy.at[pl.ds(0, Y - 1)], sy_s)

    def feedback(i):
        at = pl.ds(pl.multiple_of(i * tile, tile), tile)
        out = lax.dot_general(orth_v[...], cg[at, :], nt, preferred_element_type=F32)
        new_momentum[:, at] = (b_v[:, at].astype(F32) - (1.0 - keep_factor) * out).astype(BF16)

    feedback(y)
    for e in (1, 3, 2):
        gather_y(cg, ay_r, e)
        feedback(lax.rem(y - e + Y, Y))
    arrived(sy.at[pl.ds(0, Y - 1)], sy_r)
    total = sy[0]
    for k in range(1, Y):
        total = total + sy[k]
    scale = math.sqrt(D) * lax.rsqrt(total + norm_eps)
    new_right[...] = own[...] * scale
    scaled = (orth_v[...].astype(F32) * (math.sqrt(D / RANK) * scale)).astype(BF16)

    def outer(i):
        at = pl.ds(pl.multiple_of(i * tile, tile), tile)
        update[:, at] = lax.dot_general(scaled, cg[at, :], nt, preferred_element_type=F32).astype(BF16)

    loop(0, Y, outer)

    for wait in pending:
        wait()


def local(momentum, gradient, right_factor):
    rows, cols = momentum.shape
    chunk = right_factor.shape[0]
    F, M = lax.axis_size("fsdp"), lax.axis_size("mat")
    prows, grows = rows // M, RANK // M
    vmem, dma = pltpu.VMEM, pltpu.SemaphoreType.DMA
    whole = pl.BlockSpec(memory_space=pltpu.VMEM)
    hbm = pl.BlockSpec(memory_space=pltpu.HBM)
    ring = [dma((Z,)), dma((Z,))]
    plane = [dma((Z * Y,)), dma((Z * Y,))]
    pair = [dma((M,)), dma((M,))]
    new_right, new_momentum, update = pl.pallas_call(
        exchange,
        out_shape=(
            jax.ShapeDtypeStruct((chunk, RANK), F32),
            jax.ShapeDtypeStruct((rows, cols), BF16),
            jax.ShapeDtypeStruct((rows, cols), BF16),
        ),
        in_specs=[hbm, hbm, hbm],
        out_specs=(whole, whole, whole),
        scratch_shapes=[
            vmem((rows, cols), BF16), vmem((rows, cols), BF16), vmem((chunk, RANK), F32), vmem((cols, RANK), BF16),
            vmem((rows, cols), BF16), vmem((cols, rows), BF16),
            vmem((cols, RANK), BF16), vmem((rows, RANK), F32), vmem((M, prows, RANK), F32), vmem((rows, RANK), F32),
            vmem((RANK, RANK), F32), vmem((Y, grows, RANK), F32), vmem((Z, grows, RANK), F32),
            vmem((RANK, RANK), F32), vmem((RANK, RANK), F32), vmem((rows, RANK), BF16),
            vmem((cols, RANK), F32), vmem((Z, Y - 1, chunk, RANK), F32), vmem((Z, chunk, RANK), F32),
            vmem((Z, chunk, RANK), F32), vmem((chunk, RANK), F32), vmem((M, 1, RANK), F32), vmem((Z, 1, RANK), F32),
            vmem((Y, 1, RANK), F32),
            dma((3,)), *[dma(())] * 11, dma((Z,)), *[dma(())] * 8, *[dma(()), dma((Z,)), dma(()), dma((Y,))] * 2,
        ],
        compiler_params=pltpu.CompilerParams(
            collective_id=0, has_side_effects=True, vmem_limit_bytes=51 * 2**20
        ),
        name="exchange",
    )(momentum, gradient, right_factor)
    return (new_momentum, update, new_right)


def solution(mesh):
    placed = (P("fsdp", "mat"), P("fsdp", "mat"), P(("mat", "fsdp"), None))
    return jax.shard_map(
        local,
        mesh=mesh,
        in_specs=placed,
        out_specs=(P("fsdp", "mat"), P("fsdp", "mat"), P(("mat", "fsdp"), None)),
        check_vma=False,
    )
```

```python
import functools
import math

import jax
import jax.numpy as jnp
from jax import lax
from jax.experimental import pallas as pl
from jax.experimental.pallas import tpu as pltpu
from jax.sharding import PartitionSpec as P

D = 16384
RANK = 128
Y, Z = 4, 16

keep_factor = 0.95
norm_eps = 1e-06

MESH = pl.DeviceIdType.MESH
F32, BF16 = jnp.float32, jnp.bfloat16
HIGH = lax.Precision.HIGHEST
BLOCK = 32
EARLY = 5


def factor_inverse(a_ref, v_ref):
    n = a_ref.shape[0]
    rows = lax.broadcasted_iota(jnp.int32, (n, n), 0)
    lanes = lax.broadcasted_iota(jnp.int32, (n, n), 1)
    v_ref[...] = jnp.where(rows == lanes, 1.0, 0.0).astype(F32)
    row = lax.broadcasted_iota(jnp.int32, (BLOCK, n), 0)
    lane = lax.broadcasted_iota(jnp.int32, (BLOCK, n), 1)

    def step(j, carry):
        at = pl.ds(pl.multiple_of(j * BLOCK, BLOCK), BLOCK)
        p, v = a_ref[at, :], v_ref[at, :]
        near = pltpu.roll(p, lax.rem(n - j * BLOCK, n), 1)
        cols = [jnp.broadcast_to(near[:, k : k + 1], (BLOCK, n)) for k in range(BLOCK)]
        pivots = jnp.zeros((BLOCK, n), F32)
        for k in range(BLOCK):
            pivot = cols[k][k : k + 1, :]
            root = lax.rsqrt(pivot)
            root = root * (1.5 - 0.5 * pivot * root * root)
            mult = jnp.where(row > k, cols[k] * (root * root), 0.0)
            for other in range(k + 1, BLOCK):
                cols[other] = cols[other] - mult * cols[other][k : k + 1, :]
            p = p - mult * p[k : k + 1, :]
            v = v - mult * v[k : k + 1, :]
            pivots = jnp.where(row == k, pivot, pivots)
        scale = lax.rsqrt(pivots)
        scale = scale * (1.5 - 0.5 * pivots * scale * scale)
        p, v = p * scale, v * scale
        ahead = jnp.where(lane >= (j + 1) * BLOCK, p, 0.0)
        dims = (((0,), (0,)), ((), ()))
        a_ref[...] -= lax.dot_general(ahead, p, dims, precision=HIGH, preferred_element_type=F32)
        v_ref[...] -= lax.dot_general(ahead, v, dims, precision=HIGH, preferred_element_type=F32)
        v_ref[at, :] = v
        return carry

    lax.fori_loop(0, n // BLOCK, step, 0)


def exchange(
    mom, grad, right, new_right, new_momentum, update,
    mom_v, grad_v, right_v, cg, b_v, bt_v, rg, pp, prs, pf, gp, gy, gz, gf, inv, orth_v, cp, cy, cs, cz, own, sm, sz, sy,
    in_sem, p_s, p_r, q_s, q_r, gy_s, gy_r, gz_s, gz_r, gm_s, gm_r, cy_s, cy_r, cz_s, cz_r,
    sm_s, sm_r, sz_s, sz_r, sy_s, sy_r, rz_s, rz_r, ry_s, ry_r, az_s, az_r, ay_s, ay_r,
):
    M = prs.shape[0]
    rows, cols = b_v.shape
    chunk = cz.shape[1]
    prows = prs.shape[1]
    grows = gz.shape[1]
    F = Y * Z
    tile = cols // Y
    ring = [d for k in range(1, Z // 2) for d in (k, Z - k)] + [Z // 2]
    mats = sorted(range(1, M), key=lambda d: abs(2 * d - M))
    nt = (((1,), (1,)), ((), ()))
    f, m = lax.axis_index("fsdp"), lax.axis_index("mat")
    y, z = f // Z, f % Z

    def zpeer(d):
        return (y * Z + lax.rem(z + d, Z), m)

    def ypeer(d):
        return (lax.rem(y + d, Y) * Z + z, m)

    def mpeer(d):
        return (f, lax.rem(m + d, M))

    def part(ref, index, size):
        return ref.at[pl.ds(pl.multiple_of(index * size, size), size)]

    def copy(src, dst, send, recv, device):
        return pltpu.make_async_remote_copy(
            src_ref=src, dst_ref=dst, send_sem=send, recv_sem=recv, device_id=device, device_id_type=MESH
        )

    def arrived(ref, sem):
        copy(ref, ref, sem, sem, zpeer(1)).wait_recv()

    pending = []

    def sent(ref, sem):
        pending.append(lambda: copy(ref, ref, sem, sem, zpeer(1)).wait_send())

    barrier = pltpu.get_barrier_semaphore()
    near = Z // 4
    peers = [zpeer(d) for d in reversed(ring[: 2 * near])] + [mpeer(d) for d in range(1, M)] + [ypeer(d) for d in range(1, Y)]
    for peer in peers:
        pl.semaphore_signal(barrier, 1, device_id=peer, device_id_type=MESH)
    load_m = pltpu.make_async_copy(mom, mom_v, in_sem.at[0])
    load_g = pltpu.make_async_copy(grad, grad_v, in_sem.at[1])
    load_r = pltpu.make_async_copy(right, right_v, in_sem.at[2])
    load_r.start()
    load_m.start()
    load_g.start()
    load_r.wait()
    part(rg, f, chunk)[...] = right_v[...].astype(BF16)
    load_m.wait()
    load_g.wait()
    b_v[...] = (mom_v[...].astype(F32) + grad_v[...].astype(F32)).astype(BF16)
    pl.semaphore_wait(barrier, len(peers))

    def block_of(buf, d):
        return part(buf, y * Z + lax.rem(z - d + Z, Z), chunk)

    def along_y(buf, d, y_s, y_r):
        block = block_of(buf, d)
        for e in (2, 1, 3):
            copy(block, block, y_s, y_r.at[e], ypeer(e)).start()

    def gather_z(buf, z_s, z_r, y_s, y_r, beside):
        def along_z(d, k):
            to = (d + k) % Z
            copy(block_of(buf, d), block_of(buf, d), z_s, z_r.at[to], zpeer(k)).start()

        def take(d):
            arrived(block_of(buf, d), z_r.at[d])

        for k in range(near, 0, -1):
            along_z(0, k)
            along_z(0, Z - k)
        along_y(buf, 0, y_s, y_r)
        beside()
        first = ring[: near // 2 * 2]
        for d in first:
            take(d)
            along_y(buf, d, y_s, y_r)
        take(near)
        for k in range(near, 0, -1):
            along_z(near, k)
        take(Z - near)
        for k in range(near - 1, 0, -1):
            along_z(Z - near, Z - k)
        along_y(buf, near, y_s, y_r)
        along_y(buf, Z - near, y_s, y_r)
        for d in ring:
            if d not in (*first, near, Z - near):
                take(d)
                along_y(buf, d, y_s, y_r)
        sent(buf.at[pl.ds(0, (Z - 1) * chunk)], z_s)
        sent(buf.at[pl.ds(0, (F - Z) * chunk)], y_s)

    def gather_y(buf, y_r, e):
        arrived(buf.at[pl.ds(0, Z * chunk)], y_r.at[e])

    def turned():
        bt_v[...] = b_v[...].T

    gather_z(rg, rz_s, rz_r, ry_s, ry_r, turned)

    for e in (1, 3, 2):
        gather_y(rg, ry_r, e)
    pp[...] = jnp.dot(b_v[...], rg[...], preferred_element_type=F32)
    for d in mats:
        copy(part(pp, lax.rem(m + d, M), prows), prs.at[d], p_s, p_r, mpeer(d)).start()
    prs[0] = part(pp, m, prows)[...]
    arrived(prs.at[pl.ds(1, M - 1)], p_r)
    sent(prs.at[pl.ds(1, M - 1)], p_s)
    total = prs[0]
    for d in range(1, M):
        total = total + prs[d]
    mine = part(pf, m, prows)
    mine[...] = total
    for d in mats:
        copy(mine, mine, q_s, q_r, mpeer(d)).start()
    arrived(pf.at[pl.ds(0, (M - 1) * prows)], q_r)
    sent(pf.at[pl.ds(0, (M - 1) * prows)], q_s)

    p = pf[...]
    gp[...] = lax.dot_general(p, p, (((0,), (0,)), ((), ())), precision=HIGH, preferred_element_type=F32)
    gmine = part(gp, m, grows)

    gy[y] = gmine[...]
    for e in (2, 1, 3):
        copy(gmine, gy.at[y], gy_s, gy_r, ypeer(e)).start()
    sent(gy.at[pl.ds(0, Y - 1)], gy_s)

    p1 = p.astype(BF16)
    rest = p - p1.astype(F32)
    p2 = rest.astype(BF16)
    p3 = (rest - p2.astype(F32)).astype(BF16)
    terms = jnp.concatenate([p1, p2, p3], axis=1)
    def product(i):
        at = pl.ds(pl.multiple_of(i * tile, tile), tile)
        out = jnp.dot(bt_v[at, :], terms, preferred_element_type=F32)
        cp[at, :] = out[:, :RANK] + out[:, RANK : 2 * RANK] + out[:, 2 * RANK :]

    def loop(lo, hi, body):
        def step(i, carry):
            body(i)
            return carry

        lax.fori_loop(lo, hi, step, 0)

    loop(0, Y, product)

    def term(e, d):
        return part(cp, lax.rem(y + e, Y) * Z + lax.rem(z + d, Z), chunk)

    order = [*reversed(ring), 0]
    for d in order:
        for e in (2, 1, 3):
            copy(term(e, d), cy.at[d, e - 1], cy_s, cy_r.at[d], ypeer(e)).start()
    sent(cp.at[pl.ds(0, (F - Z) * chunk)], cy_s)

    arrived(gy.at[pl.ds(0, Y - 1)], gy_r)
    total = gy[0]
    for k in range(1, Y):
        total = total + gy[k]
    gz[z] = total
    for d in reversed(ring):
        copy(gz.at[z], gz.at[z], gz_s, gz_r, zpeer(d)).start()
    sent(gz.at[pl.ds(0, Z - 1)], gz_s)

    def combine(d):
        arrived(cy.at[d], cy_r.at[d])
        cs[d] = term(0, d)[...] + cy[d, 0] + cy[d, 1] + cy[d, 2]

    def combine_send(d):
        combine(d)
        copy(cs.at[d], cz.at[d], cz_s, cz_r, zpeer(d)).start()

    for d in order[:EARLY]:
        combine_send(d)

    arrived(gz.at[pl.ds(0, Z - 1)], gz_r)
    total = gz[0]
    for k in range(1, Z):
        total = total + gz[k]
    gown = part(gf, m, grows)
    gown[...] = total
    for d in mats:
        copy(gown, gown, gm_s, gm_r, mpeer(d)).start()
    for d in order[EARLY : Z - 1]:
        combine_send(d)
    combine(0)
    arrived(gf.at[pl.ds(0, (M - 1) * grows)], gm_r)
    copy(gf.at[pl.ds(0, (M - 1) * grows)], gown, gm_s, gm_s, zpeer(1)).wait_send()

    factor_inverse(gf, inv)
    sent(cz.at[pl.ds(0, Z - 1)], cz_s)
    linv = inv[...]

    arrived(cz.at[pl.ds(1, Z - 1)], cz_r)
    total = cs[0]
    for d in range(1, Z):
        total = total + cz[d]
    columns = lax.dot_general(total, linv, nt, precision=HIGH, preferred_element_type=F32)
    own[...] = columns
    part(cg, f, chunk)[...] = columns.astype(BF16)

    sm[m] = jnp.sum(columns * columns, axis=0, keepdims=True)

    def squares():
        for d in mats:
            copy(sm.at[m], sm.at[m], sm_s, sm_r, mpeer(d)).start()
        sent(sm.at[pl.ds(0, M - 1)], sm_s)
        orth_v[...] = lax.dot_general(pf[...], linv, nt, precision=HIGH, preferred_element_type=F32).astype(BF16)
        arrived(sm.at[pl.ds(0, M - 1)], sm_r)
        total = sm[0]
        for k in range(1, M):
            total = total + sm[k]
        sz[z] = total
        for d in reversed(ring):
            copy(sz.at[z], sz.at[z], sz_s, sz_r, zpeer(d)).start()
        sent(sz.at[pl.ds(0, Z - 1)], sz_s)

    gather_z(cg, az_s, az_r, ay_s, ay_r, squares)
    arrived(sz.at[pl.ds(0, Z - 1)], sz_r)
    total = sz[0]
    for k in range(1, Z):
        total = total + sz[k]
    sy[y] = total
    for e in (2, 1, 3):
        copy(sy.at[y], sy.at[y], sy_s, sy_r, ypeer(e)).start()
    sent(sy.at[pl.ds(0, Y - 1)], sy_s)

    def feedback(i):
        at = pl.ds(pl.multiple_of(i * tile, tile), tile)
        out = lax.dot_general(orth_v[...], cg[at, :], nt, preferred_element_type=F32)
        new_momentum[:, at] = (b_v[:, at].astype(F32) - (1.0 - keep_factor) * out).astype(BF16)

    feedback(y)
    for e in (1, 3, 2):
        gather_y(cg, ay_r, e)
        feedback(lax.rem(y - e + Y, Y))
    arrived(sy.at[pl.ds(0, Y - 1)], sy_r)
    total = sy[0]
    for k in range(1, Y):
        total = total + sy[k]
    scale = math.sqrt(D) * lax.rsqrt(total + norm_eps)
    new_right[...] = own[...] * scale
    scaled = (orth_v[...].astype(F32) * (math.sqrt(D / RANK) * scale)).astype(BF16)

    def outer(i):
        at = pl.ds(pl.multiple_of(i * tile, tile), tile)
        update[:, at] = lax.dot_general(scaled, cg[at, :], nt, preferred_element_type=F32).astype(BF16)

    loop(0, Y, outer)

    for wait in pending:
        wait()


def local(momentum, gradient, right_factor):
    rows, cols = momentum.shape
    chunk = right_factor.shape[0]
    F, M = lax.axis_size("fsdp"), lax.axis_size("mat")
    prows, grows = rows // M, RANK // M
    vmem, dma = pltpu.VMEM, pltpu.SemaphoreType.DMA
    whole = pl.BlockSpec(memory_space=pltpu.VMEM)
    hbm = pl.BlockSpec(memory_space=pltpu.HBM)
    ring = [dma((Z,)), dma((Z,))]
    plane = [dma((Z * Y,)), dma((Z * Y,))]
    pair = [dma((M,)), dma((M,))]
    new_right, new_momentum, update = pl.pallas_call(
        exchange,
        out_shape=(
            jax.ShapeDtypeStruct((chunk, RANK), F32),
            jax.ShapeDtypeStruct((rows, cols), BF16),
            jax.ShapeDtypeStruct((rows, cols), BF16),
        ),
        in_specs=[hbm, hbm, hbm],
        out_specs=(whole, whole, whole),
        scratch_shapes=[
            vmem((rows, cols), BF16), vmem((rows, cols), BF16), vmem((chunk, RANK), F32), vmem((cols, RANK), BF16),
            vmem((rows, cols), BF16), vmem((cols, rows), BF16),
            vmem((cols, RANK), BF16), vmem((rows, RANK), F32), vmem((M, prows, RANK), F32), vmem((rows, RANK), F32),
            vmem((RANK, RANK), F32), vmem((Y, grows, RANK), F32), vmem((Z, grows, RANK), F32),
            vmem((RANK, RANK), F32), vmem((RANK, RANK), F32), vmem((rows, RANK), BF16),
            vmem((cols, RANK), F32), vmem((Z, Y - 1, chunk, RANK), F32), vmem((Z, chunk, RANK), F32),
            vmem((Z, chunk, RANK), F32), vmem((chunk, RANK), F32), vmem((M, 1, RANK), F32), vmem((Z, 1, RANK), F32),
            vmem((Y, 1, RANK), F32),
            dma((3,)), *[dma(())] * 11, dma((Z,)), *[dma(())] * 8, *[dma(()), dma((Z,)), dma(()), dma((Y,))] * 2,
        ],
        compiler_params=pltpu.CompilerParams(
            collective_id=0, has_side_effects=True, vmem_limit_bytes=51 * 2**20
        ),
        name="exchange",
    )(momentum, gradient, right_factor)
    return (new_momentum, update, new_right)


def solution(mesh):
    placed = (P("fsdp", "mat"), P("fsdp", "mat"), P(("mat", "fsdp"), None))
    return jax.shard_map(
        local,
        mesh=mesh,
        in_specs=placed,
        out_specs=(P("fsdp", "mat"), P("fsdp", "mat"), P(("mat", "fsdp"), None)),
        check_vma=False,
    )
```

```python
import functools
import math

import jax
import jax.numpy as jnp
from jax import lax
from jax.experimental import pallas as pl
from jax.experimental.pallas import tpu as pltpu
from jax.sharding import PartitionSpec as P

D = 16384
RANK = 128
Y, Z = 4, 16

keep_factor = 0.95
norm_eps = 1e-06

MESH = pl.DeviceIdType.MESH
F32, BF16 = jnp.float32, jnp.bfloat16
HIGH = lax.Precision.HIGHEST
BLOCK = 32
EARLY = 5


def factor_inverse(a_ref, v_ref):
    n = a_ref.shape[0]
    rows = lax.broadcasted_iota(jnp.int32, (n, n), 0)
    lanes = lax.broadcasted_iota(jnp.int32, (n, n), 1)
    v_ref[...] = jnp.where(rows == lanes, 1.0, 0.0).astype(F32)
    row = lax.broadcasted_iota(jnp.int32, (BLOCK, n), 0)
    lane = lax.broadcasted_iota(jnp.int32, (BLOCK, n), 1)

    def step(j, carry):
        at = pl.ds(pl.multiple_of(j * BLOCK, BLOCK), BLOCK)
        p, v = a_ref[at, :], v_ref[at, :]
        near = pltpu.roll(p, lax.rem(n - j * BLOCK, n), 1)
        cols = [jnp.broadcast_to(near[:, k : k + 1], (BLOCK, n)) for k in range(BLOCK)]
        pivots = jnp.zeros((BLOCK, n), F32)
        for k in range(BLOCK):
            pivot = cols[k][k : k + 1, :]
            root = lax.rsqrt(pivot)
            root = root * (1.5 - 0.5 * pivot * root * root)
            mult = jnp.where(row > k, cols[k] * (root * root), 0.0)
            for other in range(k + 1, BLOCK):
                cols[other] = cols[other] - mult * cols[other][k : k + 1, :]
            p = p - mult * p[k : k + 1, :]
            v = v - mult * v[k : k + 1, :]
            pivots = jnp.where(row == k, pivot, pivots)
        scale = lax.rsqrt(pivots)
        scale = scale * (1.5 - 0.5 * pivots * scale * scale)
        p, v = p * scale, v * scale
        ahead = jnp.where(lane >= (j + 1) * BLOCK, p, 0.0)
        dims = (((0,), (0,)), ((), ()))
        a_ref[...] -= lax.dot_general(ahead, p, dims, precision=HIGH, preferred_element_type=F32)
        v_ref[...] -= lax.dot_general(ahead, v, dims, precision=HIGH, preferred_element_type=F32)
        v_ref[at, :] = v
        return carry

    lax.fori_loop(0, n // BLOCK, step, 0)


def exchange(
    mom, grad, right, new_right, new_momentum, update,
    mom_v, grad_v, right_v, cg, b_v, bt_v, rg, pp, prs, pf, gp, gy, gz, gf, inv, orth_v, cp, cy, cs, cz, own, sm, sz, sy,
    in_sem, p_s, p_r, q_s, q_r, gy_s, gy_r, gz_s, gz_r, gm_s, gm_r, cy_s, cy_r, cz_s, cz_r,
    sm_s, sm_r, sz_s, sz_r, sy_s, sy_r, rz_s, rz_r, ry_s, ry_r, az_s, az_r, ay_s, ay_r,
):
    M = prs.shape[0]
    rows, cols = b_v.shape
    chunk = cz.shape[1]
    prows = prs.shape[1]
    grows = gz.shape[1]
    F = Y * Z
    tile = cols // Y
    ring = [d for k in range(1, Z // 2) for d in (k, Z - k)] + [Z // 2]
    mats = sorted(range(1, M), key=lambda d: abs(2 * d - M))
    nt = (((1,), (1,)), ((), ()))
    f, m = lax.axis_index("fsdp"), lax.axis_index("mat")
    y, z = f // Z, f % Z

    def zpeer(d):
        return (y * Z + lax.rem(z + d, Z), m)

    def ypeer(d):
        return (lax.rem(y + d, Y) * Z + z, m)

    def mpeer(d):
        return (f, lax.rem(m + d, M))

    def part(ref, index, size):
        return ref.at[pl.ds(pl.multiple_of(index * size, size), size)]

    def copy(src, dst, send, recv, device):
        return pltpu.make_async_remote_copy(
            src_ref=src, dst_ref=dst, send_sem=send, recv_sem=recv, device_id=device, device_id_type=MESH
        )

    def arrived(ref, sem):
        copy(ref, ref, sem, sem, zpeer(1)).wait_recv()

    pending = []

    def sent(ref, sem):
        pending.append(lambda: copy(ref, ref, sem, sem, zpeer(1)).wait_send())

    barrier = pltpu.get_barrier_semaphore()
    near = Z // 4
    peers = [zpeer(d) for d in reversed(ring[: 2 * near])] + [mpeer(d) for d in range(1, M)] + [ypeer(d) for d in range(1, Y)]
    for peer in peers:
        pl.semaphore_signal(barrier, 1, device_id=peer, device_id_type=MESH)
    load_m = pltpu.make_async_copy(mom, mom_v, in_sem.at[0])
    load_g = pltpu.make_async_copy(grad, grad_v, in_sem.at[1])
    load_r = pltpu.make_async_copy(right, right_v, in_sem.at[2])
    load_r.start()
    load_m.start()
    load_g.start()
    load_r.wait()
    part(rg, f, chunk)[...] = right_v[...].astype(BF16)
    load_m.wait()
    load_g.wait()
    b_v[...] = (mom_v[...].astype(F32) + grad_v[...].astype(F32)).astype(BF16)
    pl.semaphore_wait(barrier, len(peers))

    def block_of(buf, d):
        return part(buf, y * Z + lax.rem(z - d + Z, Z), chunk)

    def along_y(buf, d, y_s, y_r):
        block = block_of(buf, d)
        for e in (2, 1, 3):
            copy(block, block, y_s, y_r.at[e], ypeer(e)).start()

    def gather_z(buf, z_s, z_r, y_s, y_r, beside):
        def along_z(d, k):
            to = (d + k) % Z
            copy(block_of(buf, d), block_of(buf, d), z_s, z_r.at[to], zpeer(k)).start()

        def take(d):
            arrived(block_of(buf, d), z_r.at[d])

        for k in range(near, 0, -1):
            along_z(0, k)
            along_z(0, Z - k)
        along_y(buf, 0, y_s, y_r)
        beside()
        first = ring[: near // 2 * 2]
        for d in first:
            take(d)
            along_y(buf, d, y_s, y_r)
        take(near)
        for k in range(near, 0, -1):
            along_z(near, k)
        take(Z - near)
        for k in range(near - 1, 0, -1):
            along_z(Z - near, Z - k)
        along_y(buf, near, y_s, y_r)
        along_y(buf, Z - near, y_s, y_r)
        for d in ring:
            if d not in (*first, near, Z - near):
                take(d)
                along_y(buf, d, y_s, y_r)
        sent(buf.at[pl.ds(0, (Z - 1) * chunk)], z_s)
        sent(buf.at[pl.ds(0, (F - Z) * chunk)], y_s)

    def gather_y(buf, y_r, e):
        arrived(buf.at[pl.ds(0, Z * chunk)], y_r.at[e])

    def turned():
        bt_v[...] = b_v[...].T

    gather_z(rg, rz_s, rz_r, ry_s, ry_r, turned)

    for e in (1, 3, 2):
        gather_y(rg, ry_r, e)
    pp[...] = jnp.dot(b_v[...], rg[...], preferred_element_type=F32)
    for d in mats:
        copy(part(pp, lax.rem(m + d, M), prows), prs.at[d], p_s, p_r, mpeer(d)).start()
    prs[0] = part(pp, m, prows)[...]
    arrived(prs.at[pl.ds(1, M - 1)], p_r)
    sent(prs.at[pl.ds(1, M - 1)], p_s)
    total = prs[0]
    for d in range(1, M):
        total = total + prs[d]
    mine = part(pf, m, prows)
    mine[...] = total
    for d in mats:
        copy(mine, mine, q_s, q_r, mpeer(d)).start()
    arrived(pf.at[pl.ds(0, (M - 1) * prows)], q_r)
    sent(pf.at[pl.ds(0, (M - 1) * prows)], q_s)

    p = pf[...]
    gp[...] = lax.dot_general(p, p, (((0,), (0,)), ((), ())), precision=HIGH, preferred_element_type=F32)
    gmine = part(gp, m, grows)

    gy[y] = gmine[...]
    for e in (2, 1, 3):
        copy(gmine, gy.at[y], gy_s, gy_r, ypeer(e)).start()
    sent(gy.at[pl.ds(0, Y - 1)], gy_s)

    p1 = p.astype(BF16)
    rest = p - p1.astype(F32)
    p2 = rest.astype(BF16)
    p3 = (rest - p2.astype(F32)).astype(BF16)
    terms = jnp.concatenate([p1, p2, p3], axis=1)
    def product(i):
        at = pl.ds(pl.multiple_of(i * tile, tile), tile)
        out = jnp.dot(bt_v[at, :], terms, preferred_element_type=F32)
        cp[at, :] = out[:, :RANK] + out[:, RANK : 2 * RANK] + out[:, 2 * RANK :]

    def loop(lo, hi, body):
        def step(i, carry):
            body(i)
            return carry

        lax.fori_loop(lo, hi, step, 0)

    loop(0, Y, product)

    def term(e, d):
        return part(cp, lax.rem(y + e, Y) * Z + lax.rem(z + d, Z), chunk)

    order = [*reversed(ring), 0]
    arrived(gy.at[pl.ds(0, Y - 1)], gy_r)
    total = gy[0]
    for k in range(1, Y):
        total = total + gy[k]
    gz[z] = total
    for d in reversed(ring):
        copy(gz.at[z], gz.at[z], gz_s, gz_r, zpeer(d)).start()
    sent(gz.at[pl.ds(0, Z - 1)], gz_s)

    for d in order:
        for e in (2, 1, 3):
            copy(term(e, d), cy.at[d, e - 1], cy_s, cy_r.at[d], ypeer(e)).start()
    sent(cp.at[pl.ds(0, (F - Z) * chunk)], cy_s)

    def combine(d):
        arrived(cy.at[d], cy_r.at[d])
        cs[d] = term(0, d)[...] + cy[d, 0] + cy[d, 1] + cy[d, 2]

    def combine_send(d):
        combine(d)
        copy(cs.at[d], cz.at[d], cz_s, cz_r, zpeer(d)).start()

    for d in order[:EARLY]:
        combine_send(d)

    arrived(gz.at[pl.ds(0, Z - 1)], gz_r)
    total = gz[0]
    for k in range(1, Z):
        total = total + gz[k]
    gown = part(gf, m, grows)
    gown[...] = total
    for d in mats:
        copy(gown, gown, gm_s, gm_r, mpeer(d)).start()
    for d in order[EARLY : Z - 1]:
        combine_send(d)
    combine(0)
    arrived(gf.at[pl.ds(0, (M - 1) * grows)], gm_r)
    copy(gf.at[pl.ds(0, (M - 1) * grows)], gown, gm_s, gm_s, zpeer(1)).wait_send()

    factor_inverse(gf, inv)
    sent(cz.at[pl.ds(0, Z - 1)], cz_s)
    linv = inv[...]

    arrived(cz.at[pl.ds(1, Z - 1)], cz_r)
    total = cs[0]
    for d in range(1, Z):
        total = total + cz[d]
    columns = lax.dot_general(total, linv, nt, precision=HIGH, preferred_element_type=F32)
    own[...] = columns
    part(cg, f, chunk)[...] = columns.astype(BF16)

    sm[m] = jnp.sum(columns * columns, axis=0, keepdims=True)

    def squares():
        for d in mats:
            copy(sm.at[m], sm.at[m], sm_s, sm_r, mpeer(d)).start()
        sent(sm.at[pl.ds(0, M - 1)], sm_s)
        orth_v[...] = lax.dot_general(pf[...], linv, nt, precision=HIGH, preferred_element_type=F32).astype(BF16)
        arrived(sm.at[pl.ds(0, M - 1)], sm_r)
        total = sm[0]
        for k in range(1, M):
            total = total + sm[k]
        sz[z] = total
        for d in reversed(ring):
            copy(sz.at[z], sz.at[z], sz_s, sz_r, zpeer(d)).start()
        sent(sz.at[pl.ds(0, Z - 1)], sz_s)

    gather_z(cg, az_s, az_r, ay_s, ay_r, squares)
    arrived(sz.at[pl.ds(0, Z - 1)], sz_r)
    total = sz[0]
    for k in range(1, Z):
        total = total + sz[k]
    sy[y] = total
    for e in (2, 1, 3):
        copy(sy.at[y], sy.at[y], sy_s, sy_r, ypeer(e)).start()
    sent(sy.at[pl.ds(0, Y - 1)], sy_s)

    def feedback(i):
        at = pl.ds(pl.multiple_of(i * tile, tile), tile)
        out = lax.dot_general(orth_v[...], cg[at, :], nt, preferred_element_type=F32)
        new_momentum[:, at] = (b_v[:, at].astype(F32) - (1.0 - keep_factor) * out).astype(BF16)

    feedback(y)
    for e in (1, 3, 2):
        gather_y(cg, ay_r, e)
        feedback(lax.rem(y - e + Y, Y))
    arrived(sy.at[pl.ds(0, Y - 1)], sy_r)
    total = sy[0]
    for k in range(1, Y):
        total = total + sy[k]
    scale = math.sqrt(D) * lax.rsqrt(total + norm_eps)
    new_right[...] = own[...] * scale
    scaled = (orth_v[...].astype(F32) * (math.sqrt(D / RANK) * scale)).astype(BF16)

    def outer(i):
        at = pl.ds(pl.multiple_of(i * tile, tile), tile)
        update[:, at] = lax.dot_general(scaled, cg[at, :], nt, preferred_element_type=F32).astype(BF16)

    loop(0, Y, outer)

    for wait in pending:
        wait()


def local(momentum, gradient, right_factor):
    rows, cols = momentum.shape
    chunk = right_factor.shape[0]
    F, M = lax.axis_size("fsdp"), lax.axis_size("mat")
    prows, grows = rows // M, RANK // M
    vmem, dma = pltpu.VMEM, pltpu.SemaphoreType.DMA
    whole = pl.BlockSpec(memory_space=pltpu.VMEM)
    hbm = pl.BlockSpec(memory_space=pltpu.HBM)
    ring = [dma((Z,)), dma((Z,))]
    plane = [dma((Z * Y,)), dma((Z * Y,))]
    pair = [dma((M,)), dma((M,))]
    new_right, new_momentum, update = pl.pallas_call(
        exchange,
        out_shape=(
            jax.ShapeDtypeStruct((chunk, RANK), F32),
            jax.ShapeDtypeStruct((rows, cols), BF16),
            jax.ShapeDtypeStruct((rows, cols), BF16),
        ),
        in_specs=[hbm, hbm, hbm],
        out_specs=(whole, whole, whole),
        scratch_shapes=[
            vmem((rows, cols), BF16), vmem((rows, cols), BF16), vmem((chunk, RANK), F32), vmem((cols, RANK), BF16),
            vmem((rows, cols), BF16), vmem((cols, rows), BF16),
            vmem((cols, RANK), BF16), vmem((rows, RANK), F32), vmem((M, prows, RANK), F32), vmem((rows, RANK), F32),
            vmem((RANK, RANK), F32), vmem((Y, grows, RANK), F32), vmem((Z, grows, RANK), F32),
            vmem((RANK, RANK), F32), vmem((RANK, RANK), F32), vmem((rows, RANK), BF16),
            vmem((cols, RANK), F32), vmem((Z, Y - 1, chunk, RANK), F32), vmem((Z, chunk, RANK), F32),
            vmem((Z, chunk, RANK), F32), vmem((chunk, RANK), F32), vmem((M, 1, RANK), F32), vmem((Z, 1, RANK), F32),
            vmem((Y, 1, RANK), F32),
            dma((3,)), *[dma(())] * 11, dma((Z,)), *[dma(())] * 8, *[dma(()), dma((Z,)), dma(()), dma((Y,))] * 2,
        ],
        compiler_params=pltpu.CompilerParams(
            collective_id=0, has_side_effects=True, vmem_limit_bytes=51 * 2**20
        ),
        name="exchange",
    )(momentum, gradient, right_factor)
    return (new_momentum, update, new_right)


def solution(mesh):
    placed = (P("fsdp", "mat"), P("fsdp", "mat"), P(("mat", "fsdp"), None))
    return jax.shard_map(
        local,
        mesh=mesh,
        in_specs=placed,
        out_specs=(P("fsdp", "mat"), P("fsdp", "mat"), P(("mat", "fsdp"), None)),
        check_vma=False,
    )
```
